32 devices in a mesh: term: 4 (over x, core), blk: 8 (over z, y).
Axes of the slice: x: 2, y: 2, z: 4, core: 2. Of those that a mesh axis runs over, the one named last changes fastest.
Arguments:
- wavefunction: bfloat16 [8, 8, 256, 256], P('blk'), may hold values from -6 to 6
- left_env: bfloat16 [8, 8, 256, 256], P('term', 'blk'), may hold values from -0.25 to 0.25
- right_env: bfloat16 [8, 8, 256, 256], P('term', 'blk'), may hold values from -0.25 to 0.25
- charges: int32 [8, 2], replicated, may hold values from 0 to 2
- sector_dims: int32 [8], replicated, may hold values from 192 to 256, as said below
Outputs:
- applied_once: bfloat16 [8, 8, 256, 256], P('term', 'blk')
- applied_twice: bfloat16 [8, 8, 256, 256], P('term', 'blk')
The draws below stay inside these ranges and needn't reach their ends.
Inputs may be any that keep to these rules, and one draw needn't show every extreme that they name: `sector_dims`: some sector fills its tile.
All inputs are finite; a program needn't handle non-finite values.
Results may differ from the reference program's by a relative error of at most 0.017.
Values may be sent and summed in bfloat16 or wider, within the bound.
A program may use at most 64 MiB of HBM per device.

```python
import jax
import jax.numpy as jnp
from jax import lax

TILE = 256
TERM_DEV = 2
NS = 8
TERMS = 8
N_TERM = 4


def draw_sector_dims(key, part):
    key = jax.random.fold_in(key, 7)
    first_key, second_key = jax.random.split(key)
    values = jax.random.randint(first_key, (NS,), 3 * TILE // 4, TILE + 1)
    where_full = jax.random.randint(second_key, (), 0, NS)
    return jnp.where(jnp.arange(NS) == where_full, TILE, values).astype(jnp.int32)


def set_ends(array, own_key, low, high):
    shape = array.shape
    spot = [jax.random.randint(jax.random.fold_in(own_key, axis), (), 0, shape[axis]) for axis in range(len(shape))]
    array = array.at[tuple(spot)].set(low)
    longest = shape.index(max(shape))
    spot[longest] = (spot[longest] + 1) % shape[longest]
    return array.at[tuple(spot)].set(high)


def block_scale(own_key, dims, cuts, low, high):
    factor_of = 1.0
    for axis_at, parts in cuts:
        steps = jax.random.uniform(jax.random.fold_in(jax.random.fold_in(own_key, 6), axis_at), (parts,), jnp.float32, low / len(cuts), high / len(cuts))
        factor_of = factor_of * jnp.repeat(jnp.exp(steps), dims[axis_at] // parts).reshape((-1,) + (1,) * (len(dims) - 1 - axis_at))
    return factor_of


def gaussian(key, dims, deviation, most, cuts=(), held_as=jnp.bfloat16):
    result = deviation * jax.random.normal(key, dims, jnp.float32)
    if cuts:
        result = result * block_scale(key, dims, cuts, -0.22, 0.18)
    return jnp.clip(result, -most, most).astype(held_as)


def setup_inputs(seed: int = 0) -> dict:
    key_list = jax.random.split(jax.random.key(seed), 6)
    return {
        "wavefunction": gaussian(key_list[0], (NS, NS, TILE, TILE), 1.0, 6.0, ((0, 8),)),
        "left_env": gaussian(key_list[1], (TERMS, NS, TILE, TILE), (2 * TILE) ** -0.5, 0.25, ((0, 4), (1, 8))),
        "right_env": gaussian(key_list[2], (TERMS, NS, TILE, TILE), (2 * TILE) ** -0.5, 0.25, ((0, 4), (1, 8))),
        "charges": set_ends(jax.random.randint(key_list[3], (NS, 2), 0, 3), jax.random.fold_in(key_list[3], 1), 0, 2).astype(jnp.int32),
        "sector_dims": draw_sector_dims(jax.random.fold_in(key_list[5], 71), 0),
    }


def allowed_pairs(charges):
    delta_n = charges[None, :, 0] - charges[:, None, 0]
    delta_s = charges[None, :, 1] - charges[:, None, 1]
    good = (jnp.abs(delta_n) <= 1) & (jnp.abs(delta_s) <= 1)
    return good.astype(jnp.float32)


def sector_rows(sector_dims):
    return (jnp.arange(TILE, dtype=jnp.int32)[None, :] < sector_dims[:, None]).astype(jnp.float32)


def apply_operator(vector_state, left_env, right_env, mask_full):
    left_groups = left_env.reshape(N_TERM, TERM_DEV, NS, TILE, TILE)
    right_groups = right_env.reshape(N_TERM, TERM_DEV, NS, TILE, TILE)
    group_ids = jnp.arange(N_TERM, dtype=jnp.int32)
    state_wide = vector_state.astype(jnp.float32)

    def one_group(total, pack):
        left_part, right_part, group_id = pack
        partial_value = jnp.zeros((NS, NS, TILE, TILE), jnp.float32)
        for inner in range(TERM_DEV):
            term_id = group_id * TERM_DEV + inner
            charge_move = (term_id % 3 - 1).astype(jnp.int32)
            product = jnp.einsum('iab,ijbc->ijac', left_part[inner].astype(jnp.float32), state_wide)
            product = lax.optimization_barrier(product.astype(jnp.bfloat16)).astype(jnp.float32)
            product = jnp.roll(jnp.roll(product, charge_move, axis=0), -charge_move, axis=1)
            partial_value = partial_value + jnp.einsum('ijac,jdc->ijad', product, right_part[inner].astype(jnp.float32))
        rounded = lax.optimization_barrier(partial_value.astype(jnp.bfloat16)).astype(jnp.float32)
        return total + rounded, None

    total, unused = lax.scan(one_group, jnp.zeros((NS, NS, TILE, TILE), jnp.float32), (left_groups, right_groups, group_ids))
    return (total * mask_full).astype(jnp.bfloat16)


def reference(wavefunction, left_env, right_env, charges, sector_dims):
    allowed = allowed_pairs(charges)
    live_rows = sector_rows(sector_dims)
    mask_full = allowed[:, :, None, None] * live_rows[:, None, :, None] * live_rows[None, :, None, :]
    start = (wavefunction.astype(jnp.float32) * mask_full).astype(jnp.bfloat16)
    applied_once = apply_operator(start, left_env, right_env, mask_full)
    applied_twice = apply_operator(applied_once, left_env, right_env, mask_full)
    return (applied_once, applied_twice)
```

```python
import functools

import jax
import jax.numpy as jnp
from jax import lax
from jax.experimental import pallas as pl
from jax.experimental.pallas import tpu as pltpu
from jax.sharding import PartitionSpec as P

MESH = pl.DeviceIdType.MESH


def kernel(sizes, v_in, l_in, r_in, charges, dims, out1, out2,
           L, R, V, U, Y1, Y2, prod,
           x_send, x_recv, f_send, v_send, v_recv, r_send, r_recv,
           u_send, u_recv, o_send, o_recv):
    nt, nb, ny, ni, nw, tw, tile = sizes
    ns = nb
    nz = nb // ny
    half = nt // 2
    t = lax.axis_index("term")
    b = lax.axis_index("blk")

    def role_of(term):
        return (term % 2) * half + term // 2

    def device_of(role):
        return (role % half) * 2 + role // half

    def wrap(value, size):
        return (value + size) % size

    r = role_of(t)
    z, y = b // ny, b % ny

    barrier = pltpu.get_barrier_semaphore()
    for k in range(1, nt):
        pl.semaphore_signal(barrier, inc=1, device_id=((t + k) % nt, b), device_id_type=MESH)
    for k in range(1, nb):
        pl.semaphore_signal(barrier, inc=1, device_id=(t, (b + k) % nb), device_id_type=MESH)
    for s in (-1, 1):
        pl.semaphore_signal(barrier, inc=1,
                            device_id=(device_of(wrap(r + s, nt)), wrap(b - s, nb)), device_id_type=MESH)
    pl.semaphore_wait(barrier, nt - 1 + nb - 1 + 2)

    def send(src, dst, ssem, rsem, term, blk):
        pltpu.make_async_remote_copy(
            src_ref=src, dst_ref=dst, send_sem=ssem, recv_sem=rsem,
            device_id=(term, blk), device_id_type=MESH,
        ).start()

    def done(sem):
        pltpu.make_async_copy(L.at[0], L.at[0], sem).wait()

    def place(src, dst, ssem, rsem, term, blk, here):
        @pl.when(here)
        def _():
            pltpu.make_async_copy(src, dst, rsem).start()

        @pl.when(jnp.logical_not(here))
        def _():
            send(src, dst, ssem, rsem, term, blk)

    def left_target(k):
        w = t * tw + k
        i = wrap(b + w % 3 - 1, ns)
        return (i % ni) * nw + w, device_of(i // ni)

    for k in range(tw):
        slot, term = left_target(k)
        place(l_in.at[k, 0], L.at[slot], x_send.at[k], x_recv.at[slot], term, b, term == t)

    for s in (-1, 0, 1):
        i = wrap(b + s, ns)

        @pl.when(i // ni == r)
        def _():
            slot = (s + 1) * ni + i % ni
            for off in range(nb):
                to = (b + off) % nb
                src = v_in.at[0, wrap(to + s, ns)]
                if off == 0:
                    pltpu.make_async_copy(src, V.at[slot], v_recv.at[slot]).start()
                else:
                    send(src, V.at[slot], v_send.at[(s + 1) * nb + off], v_recv.at[slot], t, to)

    for k in range(tw):
        w = t * tw + k
        pltpu.make_async_copy(r_in.at[k, 0], R.at[w], r_recv.at[w]).start()
        for off in range(1, nt):
            send(r_in.at[k, 0], R.at[w], r_send.at[k * nt + off], r_recv.at[w], (t + off) % nt, b)

    def left_source(li, w):
        bs = wrap(r * ni + li - (w % 3 - 1), ns)
        return bs // ny, bs % ny

    slots = [(li, w, li * nw + w) for li in range(ni) for w in range(nw)]

    def forward(d, carry):
        for li, w, slot in slots:
            zs, ys = left_source(li, w)

            @pl.when((y == ys) & ((z - zs == d) | (zs - z == d)))
            def _():
                done(x_recv.at[slot])

                @pl.when((z >= zs) & (z < nz - 1))
                def _():
                    send(L.at[slot], L.at[slot], f_send.at[slot, 0], x_recv.at[slot], t, b + ny)

                @pl.when((z <= zs) & (z > 0))
                def _():
                    send(L.at[slot], L.at[slot], f_send.at[slot, 1], x_recv.at[slot], t, b - ny)

                for k in range(1, ny):
                    send(L.at[slot], L.at[slot], f_send.at[slot, 1 + k], x_recv.at[slot],
                         t, z * ny + (y + k) % ny)
        return carry

    lax.fori_loop(0, nz, forward, 0)

    rows = lax.broadcasted_iota(jnp.int32, (tile, tile), 0)
    columns = lax.broadcasted_iota(jnp.int32, (tile, tile), 1)

    def mask(i, j):
        near_n = jnp.abs(charges[j, 0] - charges[i, 0]) <= 1
        near_s = jnp.abs(charges[j, 1] - charges[i, 1]) <= 1
        allowed = jnp.where(near_n & near_s, 1, 0)
        return (rows < dims[i] * allowed) & (columns < dims[j])

    for s in (-1, 0, 1):
        for li in range(ni):
            slot = (s + 1) * ni + li
            done(v_recv.at[slot])
            keep = mask(wrap(r * ni + li - s, ns), wrap(b + s, ns))
            V[slot] = jnp.where(keep, V[slot].astype(jnp.float32), 0.0).astype(jnp.bfloat16)
    for w in range(nw):
        done(r_recv.at[w])

    for li, w, slot in slots:
        zs, ys = left_source(li, w)

        @pl.when(y != ys)
        def _():
            done(x_recv.at[slot])

    def image(state, li):
        total = None
        for w in range(nw):
            left = jnp.dot(L[li * nw + w], state[(w % 3) * ni + li],
                           preferred_element_type=jnp.float32).astype(jnp.bfloat16)
            part = lax.dot_general(left, R[w], (((1,), (1,)), ((), ())),
                                   preferred_element_type=jnp.float32)
            total = part if total is None else total + part
        return jnp.where(mask(r * ni + li, b), total, 0.0).astype(jnp.bfloat16)

    def deliver(n, li, src, dst):
        place(src.at[li], dst.at[li, 0], o_send.at[n * ni + li], o_recv.at[n * ni + li], r, b, r == t)

    def next_target(li, s):
        i = wrap(r * ni + li + s, ns)
        return (s + 1) * ni + i % ni, device_of(i // ni), wrap(b - s, nb)

    for li in range(ni):
        Y1[li] = image(V, li)
        for s in (-1, 1):
            slot, term, blk = next_target(li, s)
            send(Y1.at[li], U.at[slot], u_send.at[(s + 1) * ni + li], u_recv.at[slot], term, blk)
        U[ni + li] = Y1[li]
        deliver(0, li, Y1, out1)

    for s in (-1, 1):
        for li in range(ni):
            done(u_recv.at[(s + 1) * ni + li])
    for li in range(ni):
        Y2[li] = image(U, li)
        deliver(1, li, Y2, out2)

    for k in range(tw):
        slot, term = left_target(k)

        @pl.when(term != t)
        def _():
            done(x_send.at[k])

        for off in range(1, nt):
            done(r_send.at[k * nt + off])
    for s in (-1, 0, 1):
        @pl.when(wrap(b + s, ns) // ni == r)
        def _():
            for off in range(1, nb):
                done(v_send.at[(s + 1) * nb + off])
    for li, w, slot in slots:
        zs, ys = left_source(li, w)

        @pl.when(y == ys)
        def _():
            @pl.when((z >= zs) & (z < nz - 1))
            def _():
                done(f_send.at[slot, 0])

            @pl.when((z <= zs) & (z > 0))
            def _():
                done(f_send.at[slot, 1])

            for k in range(1, ny):
                done(f_send.at[slot, 1 + k])
    for s in (-1, 1):
        for li in range(ni):
            done(u_send.at[(s + 1) * ni + li])
    for n in range(2 * ni):
        done(o_recv.at[n])

        @pl.when(r != t)
        def _():
            done(o_send.at[n])


def on_device(wavefunction, left_env, right_env, charges, sector_dims):
    nt, nb = lax.axis_size("term"), lax.axis_size("blk")
    tw, tile = left_env.shape[0], left_env.shape[-1]
    ns = wavefunction.shape[1]
    assert wavefunction.shape[0] == 1 and ns == nb
    ni, nw = ns // nt, tw * nt
    ny = 1
    while 4 * ny * ny <= nb:
        ny *= 2
    sizes = (nt, nb, ny, ni, nw, tw, tile)

    def blocks(n):
        return pltpu.VMEM((n, tile, tile), jnp.bfloat16)

    dma = pltpu.SemaphoreType.DMA
    out = jax.ShapeDtypeStruct((ni, 1, tile, tile), jnp.bfloat16)
    hbm = pl.BlockSpec(memory_space=pl.ANY)
    smem = pl.BlockSpec(memory_space=pltpu.SMEM)
    return pl.pallas_call(
        functools.partial(kernel, sizes),
        out_shape=(out, out),
        in_specs=[hbm, hbm, hbm, smem, smem],
        out_specs=(hbm, hbm),
        scratch_shapes=[
            blocks(ni * nw), blocks(nw), blocks(3 * ni), blocks(3 * ni), blocks(ni), blocks(ni), blocks(1),
            dma((tw,)), dma((ni * nw,)), dma((ni * nw, 1 + ny)),
            dma((3 * nb,)), dma((3 * ni,)), dma((tw * nt,)), dma((nw,)),
            dma((3 * ni,)), dma((3 * ni,)), dma((2 * ni,)), dma((2 * ni,)),
        ],
        compiler_params=pltpu.CompilerParams(
            collective_id=0, has_side_effects=True, vmem_limit_bytes=40 * 2**20
        ),
    )(wavefunction, left_env, right_env, charges, sector_dims)


def solution(mesh):
    placed = (
        P("blk", None, None, None),
        P("term", "blk", None, None),
        P("term", "blk", None, None),
        P(),
        P(),
    )
    return jax.shard_map(
        on_device,
        mesh=mesh,
        in_specs=placed,
        out_specs=(P("term", "blk", None, None), P("term", "blk", None, None)),
        check_vma=False,
    )
```

```python
import functools

import jax
import jax.numpy as jnp
from jax import lax
from jax.experimental import pallas as pl
from jax.experimental.pallas import tpu as pltpu
from jax.sharding import PartitionSpec as P

MESH = pl.DeviceIdType.MESH


def kernel(sizes, v_in, l_in, r_in, charges, dims, out1, out2,
           L, R, RT, V, U, Y1, Y2, prod,
           x_send, x_recv, f_send, v_send, v_recv, r_send, r_recv,
           u_send, u_recv, o_send, o_recv):
    nt, nb, ny, ni, nw, tw, tile = sizes
    ns = nb
    nz = nb // ny
    half = nt // 2
    t = lax.axis_index("term")
    b = lax.axis_index("blk")

    def role_of(term):
        return (term % 2) * half + term // 2

    def device_of(role):
        return (role % half) * 2 + role // half

    def wrap(value, size):
        return (value + size) % size

    r = role_of(t)
    z, y = b // ny, b % ny

    barrier = pltpu.get_barrier_semaphore()
    for k in range(1, nt):
        pl.semaphore_signal(barrier, inc=1, device_id=((t + k) % nt, b), device_id_type=MESH)
    for k in range(1, nb):
        pl.semaphore_signal(barrier, inc=1, device_id=(t, (b + k) % nb), device_id_type=MESH)
    for s in (-1, 1):
        pl.semaphore_signal(barrier, inc=1,
                            device_id=(device_of(wrap(r + s, nt)), wrap(b - s, nb)), device_id_type=MESH)
    pl.semaphore_wait(barrier, nt - 1 + nb - 1 + 2)

    def send(src, dst, ssem, rsem, term, blk):
        pltpu.make_async_remote_copy(
            src_ref=src, dst_ref=dst, send_sem=ssem, recv_sem=rsem,
            device_id=(term, blk), device_id_type=MESH,
        ).start()

    def done(sem, height=tile):
        whole = L.at[0, pl.ds(0, height)]
        pltpu.make_async_copy(whole, whole, sem).wait()

    cuts = 2
    part = tile // cuts

    def piece(ref, k):
        return ref.at[pl.ds(k * part, part)]

    def place(src, dst, ssem, rsem, term, blk, here):
        @pl.when(here)
        def _():
            pltpu.make_async_copy(src, dst, rsem).start()

        @pl.when(jnp.logical_not(here))
        def _():
            send(src, dst, ssem, rsem, term, blk)

    def left_target(k):
        w = t * tw + k
        i = wrap(b + w % 3 - 1, ns)
        return (i % ni) * nw + w, device_of(i // ni)

    for k in range(tw):
        slot, term = left_target(k)
        for c in range(cuts):
            place(piece(l_in.at[k, 0], c), piece(L.at[slot], c), x_send.at[k, c], x_recv.at[slot, c],
                  term, b, term == t)

    def spread(s):
        i = wrap(b + s, ns)

        @pl.when(i // ni == r)
        def _():
            slot = (s + 1) * ni + i % ni
            for off in range(nb):
                to = (b + off) % nb
                src = v_in.at[0, wrap(to + s, ns)]
                if off == 0:
                    pltpu.make_async_copy(src, V.at[slot], v_recv.at[slot]).start()
                else:
                    send(src, V.at[slot], v_send.at[(s + 1) * nb + off], v_recv.at[slot], t, to)

    def left_source(li, w):
        bs = wrap(r * ni + li - (w % 3 - 1), ns)
        return bs // ny, bs % ny

    slots = [(li, w, li * nw + w) for li in range(ni) for w in range(nw)]

    def forward(d, carry):
        for li, w, slot in slots:
            zs, ys = left_source(li, w)

            @pl.when((y == ys) & ((z - zs == d) | (zs - z == d)))
            def _():
                for c in range(cuts):
                    done(x_recv.at[slot, c], part)
                    src = piece(L.at[slot], c)

                    @pl.when((z >= zs) & (z < nz - 1))
                    def _():
                        send(src, src, f_send.at[slot, c, 0], x_recv.at[slot, c], t, b + ny)

                    @pl.when((z <= zs) & (z > 0))
                    def _():
                        send(src, src, f_send.at[slot, c, 1], x_recv.at[slot, c], t, b - ny)

                    for k in range(1, ny):
                        send(src, src, f_send.at[slot, c, 1 + k], x_recv.at[slot, c],
                             t, z * ny + (y + k) % ny)
        return carry

    spread(0)
    forward(0, 0)
    spread(-1)

    for k in range(tw):
        w = t * tw + k
        pltpu.make_async_copy(r_in.at[k, 0], R.at[w], r_recv.at[w]).start()
        for off in range(1, nt):
            send(r_in.at[k, 0], R.at[w], r_send.at[k * nt + off], r_recv.at[w], (t + off) % nt, b)

    lax.fori_loop(1, 2, forward, 0)
    spread(1)
    lax.fori_loop(2, nz, forward, 0)

    rows = lax.broadcasted_iota(jnp.int32, (tile, tile), 0)
    columns = lax.broadcasted_iota(jnp.int32, (tile, tile), 1)

    def mask(i, j):
        near_n = jnp.abs(charges[j, 0] - charges[i, 0]) <= 1
        near_s = jnp.abs(charges[j, 1] - charges[i, 1]) <= 1
        allowed = jnp.where(near_n & near_s, 1, 0)
        return (rows < dims[i] * allowed) & (columns < dims[j])

    for s in (-1, 0, 1):
        for li in range(ni):
            slot = (s + 1) * ni + li
            done(v_recv.at[slot])
            keep = mask(wrap(r * ni + li - s, ns), wrap(b + s, ns))
            V[slot] = jnp.where(keep, V[slot].astype(jnp.float32), 0.0).astype(jnp.bfloat16)
    for w in range(nw):
        done(r_recv.at[w])
        RT[w * tile:(w + 1) * tile, :] = R[w].T

    def product(state, li, w):
        prod[li, :, w * tile:(w + 1) * tile] = jnp.dot(
            L[li * nw + w], state[(w % 3) * ni + li], preferred_element_type=jnp.float32
        ).astype(jnp.bfloat16)

    for li, w, slot in slots:
        zs, ys = left_source(li, w)

        @pl.when(y == ys)
        def _():
            product(V, li, w)

    def others(d, carry):
        for li, w, slot in slots:
            zs, ys = left_source(li, w)

            @pl.when((y != ys) & ((z - zs == d) | (zs - z == d)))
            def _():
                for c in range(cuts):
                    done(x_recv.at[slot, c], part)
                product(V, li, w)
        return carry

    lax.fori_loop(0, nz, others, 0)

    def image(li):
        total = jnp.dot(prod[li], RT[...], preferred_element_type=jnp.float32)
        return jnp.where(mask(r * ni + li, b), total, 0.0).astype(jnp.bfloat16)

    def deliver(n, li, src, dst):
        place(src.at[li], dst.at[li, 0], o_send.at[n * ni + li], o_recv.at[n * ni + li], r, b, r == t)

    def next_target(li, s):
        i = wrap(r * ni + li + s, ns)
        return (s + 1) * ni + i % ni, device_of(i // ni), wrap(b - s, nb)

    for li in range(ni):
        Y1[li] = image(li)
        for s in (-1, 1):
            slot, term, blk = next_target(li, s)
            send(Y1.at[li], U.at[slot], u_send.at[(s + 1) * ni + li], u_recv.at[slot], term, blk)
        U[ni + li] = Y1[li]
        deliver(0, li, Y1, out1)

    for s in (0, -1, 1):
        for li in range(ni):
            if s:
                done(u_recv.at[(s + 1) * ni + li])
            for w in range(nw):
                if w % 3 == s + 1:
                    product(U, li, w)
    for li in range(ni):
        Y2[li] = image(li)
        deliver(1, li, Y2, out2)

    for k in range(tw):
        slot, term = left_target(k)

        @pl.when(term != t)
        def _():
            for c in range(cuts):
                done(x_send.at[k, c], part)

        for off in range(1, nt):
            done(r_send.at[k * nt + off])
    for s in (-1, 0, 1):
        @pl.when(wrap(b + s, ns) // ni == r)
        def _():
            for off in range(1, nb):
                done(v_send.at[(s + 1) * nb + off])
    for li, w, slot in slots:
        zs, ys = left_source(li, w)

        @pl.when(y == ys)
        def _():
            for c in range(cuts):
                @pl.when((z >= zs) & (z < nz - 1))
                def _():
                    done(f_send.at[slot, c, 0], part)

                @pl.when((z <= zs) & (z > 0))
                def _():
                    done(f_send.at[slot, c, 1], part)

                for k in range(1, ny):
                    done(f_send.at[slot, c, 1 + k], part)
    for s in (-1, 1):
        for li in range(ni):
            done(u_send.at[(s + 1) * ni + li])
    for n in range(2 * ni):
        done(o_recv.at[n])

        @pl.when(r != t)
        def _():
            done(o_send.at[n])


def on_device(wavefunction, left_env, right_env, charges, sector_dims):
    nt, nb = lax.axis_size("term"), lax.axis_size("blk")
    tw, tile = left_env.shape[0], left_env.shape[-1]
    ns = wavefunction.shape[1]
    assert wavefunction.shape[0] == 1 and ns == nb
    ni, nw = ns // nt, tw * nt
    ny = 1
    while 4 * ny * ny <= nb:
        ny *= 2
    sizes = (nt, nb, ny, ni, nw, tw, tile)

    def blocks(n):
        return pltpu.VMEM((n, tile, tile), jnp.bfloat16)

    dma = pltpu.SemaphoreType.DMA
    out = jax.ShapeDtypeStruct((ni, 1, tile, tile), jnp.bfloat16)
    hbm = pl.BlockSpec(memory_space=pltpu.HBM)
    smem = pl.BlockSpec(memory_space=pltpu.SMEM)
    vmem = pl.BlockSpec(memory_space=pltpu.VMEM)
    return pl.pallas_call(
        functools.partial(kernel, sizes),
        out_shape=(out, out),
        in_specs=[hbm, hbm, hbm, smem, smem],
        out_specs=(hbm, hbm),
        scratch_shapes=[
            blocks(ni * nw), blocks(nw), pltpu.VMEM((nw * tile, tile), jnp.bfloat16), blocks(3 * ni), blocks(3 * ni), blocks(ni), blocks(ni),
            pltpu.VMEM((ni, tile, nw * tile), jnp.bfloat16),
            dma((tw, 2)), dma((ni * nw, 2)), dma((ni * nw, 2, 1 + ny)),
            dma((3 * nb,)), dma((3 * ni,)), dma((tw * nt,)), dma((nw,)),
            dma((3 * ni,)), dma((3 * ni,)), dma((2 * ni,)), dma((2 * ni,)),
        ],
        compiler_params=pltpu.CompilerParams(
            collective_id=0, has_side_effects=True, vmem_limit_bytes=60 * 2**20
        ),
    )(wavefunction, left_env, right_env, charges, sector_dims)


def solution(mesh):
    placed = (
        P("blk", None, None, None),
        P("term", "blk", None, None),
        P("term", "blk", None, None),
        P(),
        P(),
    )
    return jax.shard_map(
        on_device,
        mesh=mesh,
        in_specs=placed,
        out_specs=(P("term", "blk", None, None), P("term", "blk", None, None)),
        check_vma=False,
    )
```

```python
import functools

import jax
import jax.numpy as jnp
from jax import lax
from jax.experimental import pallas as pl
from jax.experimental.pallas import tpu as pltpu
from jax.sharding import PartitionSpec as P

MESH = pl.DeviceIdType.MESH


def kernel(sizes, v_in, l_in, r_in, charges, dims, out1, out2,
           L, R, RT, V, U, Y1, Y2, prod,
           x_send, x_recv, f_send, v_send, v_recv, r_send, r_recv,
           u_send, u_recv, o_send, o_recv):
    nt, nb, ny, ni, nw, tw, tile = sizes
    ns = nb
    nz = nb // ny
    half = nt // 2
    t = lax.axis_index("term")
    b = lax.axis_index("blk")

    def role_of(term):
        return (term % 2) * half + term // 2

    def device_of(role):
        return (role % half) * 2 + role // half

    def wrap(value, size):
        return (value + size) % size

    r = role_of(t)
    z, y = b // ny, b % ny

    barrier = pltpu.get_barrier_semaphore()
    for k in range(1, nt):
        pl.semaphore_signal(barrier, inc=1, device_id=((t + k) % nt, b), device_id_type=MESH)
    for k in range(1, nb):
        pl.semaphore_signal(barrier, inc=1, device_id=(t, (b + k) % nb), device_id_type=MESH)
    for s in (-1, 1):
        pl.semaphore_signal(barrier, inc=1,
                            device_id=(device_of(wrap(r + s, nt)), wrap(b - s, nb)), device_id_type=MESH)
    pl.semaphore_wait(barrier, nt - 1 + nb - 1 + 2)

    def send(src, dst, ssem, rsem, term, blk):
        pltpu.make_async_remote_copy(
            src_ref=src, dst_ref=dst, send_sem=ssem, recv_sem=rsem,
            device_id=(term, blk), device_id_type=MESH,
        ).start()

    def done(sem, height=tile):
        whole = L.at[0, pl.ds(0, height)]
        pltpu.make_async_copy(whole, whole, sem).wait()

    cuts = 2
    part = tile // cuts

    def piece(ref, k):
        return ref.at[pl.ds(k * part, part)]

    def place(src, dst, ssem, rsem, term, blk, here):
        @pl.when(here)
        def _():
            pltpu.make_async_copy(src, dst, rsem).start()

        @pl.when(jnp.logical_not(here))
        def _():
            send(src, dst, ssem, rsem, term, blk)

    def left_target(k):
        w = t * tw + k
        i = wrap(b + w % 3 - 1, ns)
        return (i % ni) * nw + w, device_of(i // ni)

    for k in range(tw):
        slot, term = left_target(k)
        for c in range(cuts):
            place(piece(l_in.at[k, 0], c), piece(L.at[slot], c), x_send.at[k, c], x_recv.at[slot, c],
                  term, b, term == t)

    def spread(s):
        i = wrap(b + s, ns)

        @pl.when(i // ni == r)
        def _():
            slot = (s + 1) * ni + i % ni
            for off in range(nb):
                to = (b + off) % nb
                src = v_in.at[0, wrap(to + s, ns)]
                if off == 0:
                    pltpu.make_async_copy(src, V.at[slot], v_recv.at[slot]).start()
                else:
                    send(src, V.at[slot], v_send.at[(s + 1) * nb + off], v_recv.at[slot], t, to)

    def left_source(li, w):
        bs = wrap(r * ni + li - (w % 3 - 1), ns)
        return bs // ny, bs % ny

    slots = [(li, w, li * nw + w) for li in range(ni) for w in range(nw)]

    def forward(d, carry):
        for li, w, slot in slots:
            zs, ys = left_source(li, w)

            @pl.when((y == ys) & ((z - zs == d) | (zs - z == d)))
            def _():
                for c in range(cuts):
                    done(x_recv.at[slot, c], part)
                    src = piece(L.at[slot], c)

                    @pl.when((z >= zs) & (z < nz - 1))
                    def _():
                        send(src, src, f_send.at[slot, c, 0], x_recv.at[slot, c], t, b + ny)

                    @pl.when((z <= zs) & (z > 0))
                    def _():
                        send(src, src, f_send.at[slot, c, 1], x_recv.at[slot, c], t, b - ny)

                    for k in range(1, ny):
                        send(src, src, f_send.at[slot, c, 1 + k], x_recv.at[slot, c],
                             t, z * ny + (y + k) % ny)
        return carry

    spread(0)
    forward(0, 0)
    spread(-1)

    lax.fori_loop(1, 2, forward, 0)
    spread(1)

    for k in range(tw):
        w = t * tw + k
        pltpu.make_async_copy(r_in.at[k, 0], R.at[w], r_recv.at[w]).start()
        for off in range(1, nt):
            send(r_in.at[k, 0], R.at[w], r_send.at[k * nt + off], r_recv.at[w], (t + off) % nt, b)

    lax.fori_loop(2, nz, forward, 0)

    rows = lax.broadcasted_iota(jnp.int32, (tile, tile), 0)
    columns = lax.broadcasted_iota(jnp.int32, (tile, tile), 1)

    def mask(i, j):
        near_n = jnp.abs(charges[j, 0] - charges[i, 0]) <= 1
        near_s = jnp.abs(charges[j, 1] - charges[i, 1]) <= 1
        allowed = jnp.where(near_n & near_s, 1, 0)
        return (rows < dims[i] * allowed) & (columns < dims[j])

    for s in (-1, 0, 1):
        for li in range(ni):
            slot = (s + 1) * ni + li
            done(v_recv.at[slot])
            keep = mask(wrap(r * ni + li - s, ns), wrap(b + s, ns))
            V[slot] = jnp.where(keep, V[slot].astype(jnp.float32), 0.0).astype(jnp.bfloat16)
    for w in range(nw):
        done(r_recv.at[w])
        RT[w * tile:(w + 1) * tile, :] = R[w].T

    def product(state, li, w):
        prod[li, :, w * tile:(w + 1) * tile] = jnp.dot(
            L[li * nw + w], state[(w % 3) * ni + li], preferred_element_type=jnp.float32
        ).astype(jnp.bfloat16)

    for li, w, slot in slots:
        zs, ys = left_source(li, w)

        @pl.when(y == ys)
        def _():
            product(V, li, w)

    def others(d, carry):
        for li, w, slot in slots:
            zs, ys = left_source(li, w)

            @pl.when((y != ys) & ((z - zs == d) | (zs - z == d)))
            def _():
                for c in range(cuts):
                    done(x_recv.at[slot, c], part)
                product(V, li, w)
        return carry

    lax.fori_loop(0, nz, others, 0)

    def image(li):
        total = jnp.dot(prod[li], RT[...], preferred_element_type=jnp.float32)
        return jnp.where(mask(r * ni + li, b), total, 0.0).astype(jnp.bfloat16)

    def deliver(n, li, src, dst):
        place(src.at[li], dst.at[li, 0], o_send.at[n * ni + li], o_recv.at[n * ni + li], r, b, r == t)

    def next_target(li, s):
        i = wrap(r * ni + li + s, ns)
        return (s + 1) * ni + i % ni, device_of(i // ni), wrap(b - s, nb)

    for li in range(ni):
        Y1[li] = image(li)
        for s in (-1, 1):
            slot, term, blk = next_target(li, s)
            send(Y1.at[li], U.at[slot], u_send.at[(s + 1) * ni + li], u_recv.at[slot], term, blk)
        U[ni + li] = Y1[li]
        deliver(0, li, Y1, out1)

    for s in (0, -1, 1):
        for li in range(ni):
            if s:
                done(u_recv.at[(s + 1) * ni + li])
            for w in range(nw):
                if w % 3 == s + 1:
                    product(U, li, w)
    for li in range(ni):
        Y2[li] = image(li)
        deliver(1, li, Y2, out2)

    for k in range(tw):
        slot, term = left_target(k)

        @pl.when(term != t)
        def _():
            for c in range(cuts):
                done(x_send.at[k, c], part)

        for off in range(1, nt):
            done(r_send.at[k * nt + off])
    for s in (-1, 0, 1):
        @pl.when(wrap(b + s, ns) // ni == r)
        def _():
            for off in range(1, nb):
                done(v_send.at[(s + 1) * nb + off])
    for li, w, slot in slots:
        zs, ys = left_source(li, w)

        @pl.when(y == ys)
        def _():
            for c in range(cuts):
                @pl.when((z >= zs) & (z < nz - 1))
                def _():
                    done(f_send.at[slot, c, 0], part)

                @pl.when((z <= zs) & (z > 0))
                def _():
                    done(f_send.at[slot, c, 1], part)

                for k in range(1, ny):
                    done(f_send.at[slot, c, 1 + k], part)
    for s in (-1, 1):
        for li in range(ni):
            done(u_send.at[(s + 1) * ni + li])
    for n in range(2 * ni):
        done(o_recv.at[n])

        @pl.when(r != t)
        def _():
            done(o_send.at[n])


def on_device(wavefunction, left_env, right_env, charges, sector_dims):
    nt, nb = lax.axis_size("term"), lax.axis_size("blk")
    tw, tile = left_env.shape[0], left_env.shape[-1]
    ns = wavefunction.shape[1]
    assert wavefunction.shape[0] == 1 and ns == nb
    ni, nw = ns // nt, tw * nt
    ny = 1
    while 4 * ny * ny <= nb:
        ny *= 2
    sizes = (nt, nb, ny, ni, nw, tw, tile)

    def blocks(n):
        return pltpu.VMEM((n, tile, tile), jnp.bfloat16)

    dma = pltpu.SemaphoreType.DMA
    out = jax.ShapeDtypeStruct((ni, 1, tile, tile), jnp.bfloat16)
    hbm = pl.BlockSpec(memory_space=pltpu.HBM)
    smem = pl.BlockSpec(memory_space=pltpu.SMEM)
    vmem = pl.BlockSpec(memory_space=pltpu.VMEM)
    return pl.pallas_call(
        functools.partial(kernel, sizes),
        out_shape=(out, out),
        in_specs=[hbm, hbm, hbm, smem, smem],
        out_specs=(hbm, hbm),
        scratch_shapes=[
            blocks(ni * nw), blocks(nw), pltpu.VMEM((nw * tile, tile), jnp.bfloat16), blocks(3 * ni), blocks(3 * ni), blocks(ni), blocks(ni),
            pltpu.VMEM((ni, tile, nw * tile), jnp.bfloat16),
            dma((tw, 2)), dma((ni * nw, 2)), dma((ni * nw, 2, 1 + ny)),
            dma((3 * nb,)), dma((3 * ni,)), dma((tw * nt,)), dma((nw,)),
            dma((3 * ni,)), dma((3 * ni,)), dma((2 * ni,)), dma((2 * ni,)),
        ],
        compiler_params=pltpu.CompilerParams(
            collective_id=0, has_side_effects=True, vmem_limit_bytes=60 * 2**20
        ),
    )(wavefunction, left_env, right_env, charges, sector_dims)


def solution(mesh):
    placed = (
        P("blk", None, None, None),
        P("term", "blk", None, None),
        P("term", "blk", None, None),
        P(),
        P(),
    )
    return jax.shard_map(
        on_device,
        mesh=mesh,
        in_specs=placed,
        out_specs=(P("term", "blk", None, None), P("term", "blk", None, None)),
        check_vma=False,
    )
```
